512 devices in a mesh: tile: 128 (over y, z, core), fit: 4 (over x).
Axes of the slice: x: 4, y: 4, z: 16, core: 2. Of those that a mesh axis runs over, the one named last changes fastest.
Arguments:
- factors: bfloat16 [128, 128, 128, 128], P('tile', 'fit'), may hold values from -0.21875 to 0.21875
- amplitudes: bfloat16 [256, 128, 128], P('tile'), may hold values from -6 to 6
- left_step: int32 [256, 13], P('tile'), may hold values from -1 to 1
- right_step: int32 [256, 13], P('tile'), may hold values from -1 to 1
- amp_owner: int32 [256, 13], P('tile'), may hold values from 0 to 127, all different within a row; in each aligned block of 2 rows (0 to 1, 2 to 3, ...) no two rows name the same one
- amp_slot: int32 [256, 13], P('tile'), may hold values from 0 to 1
Outputs:
- residual: bfloat16 [256, 128, 128], P('tile', 'fit')
The draws below stay inside these ranges and needn't reach their ends.
Inputs may be any that keep to these rules, and one draw needn't show every extreme that they name: `amp_owner`: among the 13 terms of the 2 residual tiles of one device, no owner index is named more than 1 times, a bound that some block reaches.
All inputs are finite; a program needn't handle non-finite values.
Results may differ from the reference program's by a relative error of at most 0.0049.
Values may be sent and summed in bfloat16 or wider, within the bound.
A program may use at most 64 MiB of HBM per device.

```python
import math
import jax
import jax.numpy as jnp
import numpy as np
from jax import lax

W = 128
NAUX = 128
NZ_DEV = 2
TERMS = 13
NF = 128
NNZ = 256
CAP = 1
N_TILE = 128


def plant(drawn, own_key, smallest, high):
    place = [jax.random.randint(jax.random.fold_in(own_key, axis), (), 0, length) for axis, length in enumerate(drawn.shape)]
    main_axis = drawn.shape.index(max(drawn.shape))
    next_to = place[:main_axis] + [(place[main_axis] + 1) % drawn.shape[main_axis]] + place[main_axis + 1:]
    return drawn.at[tuple(place)].set(smallest).at[tuple(next_to)].set(high)


def shard_levels(stream_key, extent, pieces, smallest, high):
    loudness = 1.0
    for dim, shards_of in pieces:
        draws = jax.random.uniform(jax.random.fold_in(jax.random.fold_in(stream_key, 6), dim), (shards_of,), jnp.float32, smallest / len(pieces), high / len(pieces))
        loudness = loudness * jnp.repeat(jnp.exp(draws), extent[dim] // shards_of).reshape((-1,) + (1,) * (len(extent) - 1 - dim))
    return loudness


def shared_out(stream_key, own, number, rows, amount, top, limit, lean):
    ranking = jax.random.permutation(stream_key, amount)
    heavy_load, ordinary = load_shares(amount, rows * top, limit, lean, True), load_shares(amount, rows * top, limit, lean, False)
    places = jnp.arange(amount)

    def named(lengths, rotation):
        used = int((lengths > 0).sum())
        fixed = max(1, used // 4)
        passed = fixed + (places - fixed + rotation * (used - fixed)) % max(1, amount - fixed)
        return jnp.zeros((amount,), jnp.int32).at[ranking[jnp.where(places < fixed, places, passed)]].set(jnp.asarray(lengths, jnp.int32))

    lengths = jnp.where(number % 4 == 0, named(heavy_load, number // 4), named(ordinary, number - number // 4 - 1))
    mixed = jax.random.permutation(jax.random.fold_in(own, 3), amount)
    source_of, receiver = mixed[0:amount // 2 * 2:2], mixed[1:amount // 2 * 2:2]
    room = jnp.minimum(lengths[source_of] - 1, limit - lengths[receiver]) // 2
    room = jnp.where((source_of == ranking[0]) | (receiver == ranking[0]) | (lengths[receiver] == 0), 0, jnp.maximum(room, 0))
    passed = jax.random.randint(jax.random.fold_in(own, 4), (amount // 2,), 0, 1 << 20) % (room + 1)
    lengths = lengths.at[source_of].add(-passed).at[receiver].add(passed)
    members = jnp.searchsorted(jnp.cumsum(lengths), jnp.arange(rows * top), side="right").astype(jnp.int32)
    listing = members.reshape(top, rows).T
    listing = listing[jax.random.permutation(jax.random.fold_in(own, 1), rows)]
    rotation = jax.random.randint(jax.random.fold_in(own, 2), (rows, 1), 0, top)
    return jnp.take_along_axis(listing, (jnp.arange(top)[None, :] + rotation) % top, axis=1)


def load_shares(count, total, limit, slope, full):
    loads = [(1 << 20) // math.isqrt(grade ** slope) + 1 for grade in range(1, count + 1)]
    largest = limit if full else min(limit, max(-(-total // count), total * loads[0] // sum(loads)))
    least = 1 if total - largest >= count - 1 else 0
    given, spare = [largest] + [least] * (count - 1), total - largest - least * (count - 1)
    while spare > 0:
        movable = [i for i in range(1, count) if given[i] < largest] or [i for i in range(1, count) if given[i] < limit]
        mass, budget = sum([loads[i] for i in movable]), spare
        for i in movable:
            extra = min(limit - given[i], max(1, budget * loads[i] // mass), spare)
            given[i] = given[i] + extra
            spare = spare - extra
    return np.array(given)


def centred(key, extent, spread, bound, pieces=(), dtype=jnp.bfloat16):
    array = spread * jax.random.normal(key, extent, jnp.float32)
    if pieces:
        array = array * shard_levels(key, extent, pieces, -0.22, 0.18)
    return jnp.clip(array, -bound, bound).astype(dtype)


def setup_inputs(seed: int = 0) -> dict:
    keys = jax.random.split(jax.random.key(seed), 7)
    factors = centred(keys[0], (NF, NAUX, W, W), ((W * W * NAUX * TERMS) ** -0.25), 0.21875, ((0, 128), (1, 4)))
    amplitudes = centred(keys[1], (NNZ, W, W), 1.0, 6.0, ((0, 128),))
    left_step = plant(jax.random.randint(keys[2], (NNZ, TERMS), -1, 2), jax.random.fold_in(keys[2], 1), -1, 1).astype(jnp.int32)
    right_step = plant(jax.random.randint(keys[3], (NNZ, TERMS), -1, 2), jax.random.fold_in(keys[3], 1), -1, 1).astype(jnp.int32)
    amp_owner_keys = jax.random.split(jax.random.fold_in(keys[4], 1), NNZ // NZ_DEV)
    amp_owner_turns = jax.random.permutation(jax.random.fold_in(keys[4], 3), NNZ // NZ_DEV)
    amp_owner = jax.vmap(lambda own, number: shared_out(jax.random.fold_in(keys[4], 2), own, number, NZ_DEV, N_TILE, TERMS, CAP, 2))(amp_owner_keys, amp_owner_turns).reshape((NNZ, TERMS))
    amp_slot = plant(jax.random.randint(keys[5], (NNZ, TERMS), 0, NZ_DEV), jax.random.fold_in(keys[5], 1), 0, NZ_DEV - 1).astype(jnp.int32)
    return {"factors": factors, "amplitudes": amplitudes, "left_step": left_step, "right_step": right_step, "amp_owner": amp_owner, "amp_slot": amp_slot}


def reference(factors, amplitudes, left_step, right_step, amp_owner, amp_slot):
    owner_row = (jnp.arange(NNZ) // NZ_DEV).astype(jnp.int32)[:, None]
    left_tile = jnp.clip(owner_row + left_step, 0, NF - 1).astype(jnp.int32)
    right_tile = jnp.clip(owner_row + right_step, 0, NF - 1).astype(jnp.int32)
    source = (amp_owner * NZ_DEV + amp_slot).astype(jnp.int32)

    def one_tile(ids):
        left_row, right_row, source_row = ids

        def add_term(total, item):
            left_id, right_id, source_id = item
            right_fac = factors[right_id].astype(jnp.float32)
            left_fac = factors[left_id].astype(jnp.float32)
            ampl = amplitudes[source_id].astype(jnp.float32)
            half = jnp.einsum("cd,pbd->pcb", ampl, right_fac).astype(jnp.bfloat16)
            term = jnp.einsum("pac,pcb->ab", left_fac, half.astype(jnp.float32))
            return total + term, None

        total, _ = lax.scan(add_term, jnp.zeros((W, W), jnp.float32), (left_row, right_row, source_row))
        return total.astype(jnp.bfloat16)

    return lax.map(one_tile, (left_tile, right_tile, source))
```

```python
import jax
import jax.numpy as jnp
from jax import lax
from jax.experimental import pallas as pl
from jax.experimental.pallas import tpu as pltpu
from jax.sharding import PartitionSpec as P

NX, NY, NZ, NC = 4, 4, 16, 2
TILES = NY * NZ * NC
W = 128
PAUX = 32
FAR = (0, 5, -5)
NEAR = (1, -1, 2, -2)
CHUNKS = 8
PSTEP = 4
HEAD = 80
BF16, F32 = jnp.bfloat16, jnp.float32


def remote(src, dst, send, recv, device):
    return pltpu.make_async_remote_copy(
        src_ref=src,
        dst_ref=dst,
        send_sem=send,
        recv_sem=recv,
        device_id=device,
        device_id_type=pl.DeviceIdType.MESH,
    )


def kernel(
    fac, amp, lstep, rstep, own, slot, out,
    amp_v, idx_v, code, pack, marks, wide, spread, tiles, picked, landed, amat, fcat, part, parts,
    loc, s1s, s1r, ms, mr, s2s, s2r, cs, cr, s4s, s4r, fs, fr, rs, rr,
):
    t = lax.axis_index("tile")
    x = lax.axis_index("fit")
    c = lax.rem(t, NC)
    z = lax.rem(t // NC, NZ)
    y = t // (NC * NZ)

    def at(dx, dy, dz, dc):
        yy, zz = lax.rem(y + dy + NY, NY), lax.rem(z + dz + NZ, NZ)
        return ((yy * NZ + zz) * NC + lax.rem(c + dc, NC), lax.rem(x + dx, NX))

    before = (lax.rem(t + TILES - 1, TILES), x)
    after = (lax.rem(t + 1, TILES), x)
    cross = jnp.where(c == 0, before[0], after[0])

    loads = [pltpu.make_async_copy(amp, amp_v, loc.at[0])]
    for i, ref in enumerate((lstep, rstep, own, slot)):
        loads.append(pltpu.make_async_copy(ref, idx_v.at[i], loc.at[1 + i]))
    keep = pltpu.make_async_copy(fac, fcat.at[:, pl.ds(W, W)], loc.at[5])
    for copy in loads:
        copy.start()
    keep.start()

    barrier = pltpu.get_barrier_semaphore()
    peers = []
    for dy in range(NY):
        for dz in FAR:
            if dy or dz:
                peers.append(at(0, dy, dz, 0))
    for dz in (1, -1, 2, -2, 3, -3):
        peers.append(at(0, 0, dz, 0))
    peers.append(at(0, 0, 0, 1))
    for dx in range(1, NX):
        for dy in range(NY):
            peers.append(at(dx, dy, 0, 0))
    peers.append((cross, x))
    for peer in peers:
        pl.semaphore_signal(barrier, inc=1, device_id=peer, device_id_type=pl.DeviceIdType.MESH)

    for copy in loads:
        copy.wait()

    rows = amp_v[:, pl.ds(pl.multiple_of(x * 32, 32), 32), :].astype(F32).reshape(2, NY, 8, W)
    for dest in range(NY):
        pack[dest] = rows[:, dest].reshape(16, W).astype(BF16)

    lpos = jnp.clip(t + idx_v[0], 0, TILES - 1) - t + 1
    rpos = jnp.clip(t + idx_v[1], 0, TILES - 1) - t + 1
    owner = idx_v[2]
    tile = (((owner & 1) * NZ + ((owner >> 1) & (NZ - 1))) * NY + (owner >> 5)) * 2 + idx_v[3]
    terms = lpos.shape[1]
    code[...] = jnp.full(code.shape, -1, jnp.int32)
    code[0, 0:2, 0:terms] = lpos * 3 + rpos
    code[1, 0:2, 0:terms] = tile
    for s in range(2):
        block_of = (lax.broadcasted_iota(jnp.int32, (16, W), 0) == code[0, s : s + 1, :]).astype(BF16)
        tile_of = (lax.broadcasted_iota(jnp.int32, (256, W), 0) == code[1, s : s + 1, :]).astype(BF16)
        both = lax.dot_general(block_of, tile_of, (((1,), (1,)), ((), ())), preferred_element_type=F32)
        marks[y, 16 * s : 16 * (s + 1), :] = both.astype(BF16)
    spread[...] = (
        lax.broadcasted_iota(jnp.int32, (256, 2048), 1) // 8 == lax.broadcasted_iota(jnp.int32, (256, 2048), 0)
    ).astype(BF16)

    pl.semaphore_wait(barrier, len(peers))

    sent = []
    first = {}
    for dz in (5, -5, 0):
        for dy in range(NY):
            j = FAR.index(dz) * NY + dy
            dst = lax.rem(y + dy, NY)
            if dy or dz:
                first[dz, dy] = remote(pack.at[dst], tiles.at[c, z, y], s1s.at[j], s1r.at[j], at(0, dy, dz, 0))
                first[dz, dy].start()
                sent.append(first[dz, dy])
            else:
                mine = pltpu.make_async_copy(pack.at[dst], tiles.at[c, z, y], loc.at[6])
                mine.start()
    for dy in range(1, NY):
        copy = remote(marks.at[y], marks.at[y], ms.at[dy], mr.at[dy], at(0, dy, 0, 0))
        copy.start()
        sent.append(copy)

    def arrived(dz, dy):
        j = FAR.index(dz) * NY + dy
        zz, yy = lax.rem(z - dz + NZ, NZ), lax.rem(y - dy + NY, NY)
        here = tiles.at[c, zz, yy]
        remote(here, here, s1s.at[j], s1r.at[j], after).wait_recv()

    def tile_block(dz):
        return tiles.at[c, lax.rem(z - dz + 2 * NZ, NZ)]

    partner = at(0, 0, 0, 1)

    def share(dz):
        j = dz + 7
        copy = remote(tile_block(dz), tile_block(dz), cs.at[j], cr.at[j], partner)
        copy.start()
        sent.append(copy)

    near = []
    for i, dz in enumerate(FAR):
        for dy in range(NY):
            if dy or dz:
                arrived(dz, dy)
        if dz == 0:
            mine.wait()
        steps = NEAR + ((3,) if dz == 5 else ())
        for k, step in enumerate(steps):
            j = i * 5 + k
            copy = remote(tile_block(dz), tile_block(dz), s2s.at[j], s2r.at[j], at(0, 0, step, 0))
            copy.start()
            sent.append(copy)
            near.append((j, dz + step))
        share(dz)

    for dy in range(1, NY):
        here = marks.at[lax.rem(y - dy + NY, NY)]
        remote(here, here, ms.at[dy], mr.at[dy], after).wait_recv()
    row = lax.broadcasted_iota(jnp.int32, (144, 32), 0) // 8
    col = lax.broadcasted_iota(jnp.int32, (144, 32), 1)
    rowpick = (jnp.where(row >= 9, row + 7, row) == col).astype(BF16)
    same = (lax.broadcasted_iota(jnp.int32, (144, 2048), 0) & 7) == (
        lax.broadcasted_iota(jnp.int32, (144, 2048), 1) & 7
    )
    for dest in range(NY):
        blocks = jnp.dot(rowpick, marks[dest], preferred_element_type=F32).astype(BF16)
        full = jnp.dot(blocks, spread[...], preferred_element_type=F32)
        wide[dest] = jnp.where(same, full, 0.0).astype(BF16)

    for j, dz in near:
        remote(tile_block(dz), tile_block(dz), s2s.at[j], s2r.at[j], after).wait_recv()
        share(dz)
    for dz in range(-7, 9):
        here = tiles.at[1 - c, lax.rem(z - dz + 2 * NZ, NZ)]
        remote(here, here, cs.at[dz + 7], cr.at[dz + 7], after).wait_recv()

    gathered = tiles[...].reshape(2048, W)
    picked[...] = (
        jnp.dot(wide[...].reshape(NY * 144, 2048), gathered, preferred_element_type=F32)
        .astype(BF16)
        .reshape(NY, 144, W)
    )

    def part_of(ref, half):
        return ref.at[pl.ds(0, HEAD)] if half == 0 else ref.at[pl.ds(HEAD, 144 - HEAD)]

    place = x * NY + y
    for half in range(2):
        for dx in range(NX):
            for dy in range(NY):
                dst = lax.rem(y + dy, NY)
                src_ref, dst_ref = part_of(picked.at[dst], half), part_of(landed.at[place], half)
                j = dx * NY + dy
                if dx or dy:
                    copy = remote(src_ref, dst_ref, s4s.at[half, j], s4r.at[half, j], at(dx, dy, 0, 0))
                    sent.append(copy)
                else:
                    copy = pltpu.make_async_copy(src_ref, dst_ref, s4s.at[half, 0])
                copy.start()

    count = PAUX * W // CHUNKS
    for i in range(CHUNKS):
        part_rows = pl.ds(i * count, count)
        for k, (device, lane) in enumerate(((after, 0), (before, 2 * W))):
            copy = remote(fac.at[part_rows], fcat.at[part_rows, pl.ds(lane, W)], fs.at[k, i], fr.at[k, i], device)
            copy.start()
            sent.append(copy)

    def landed_half(half):
        pltpu.make_async_copy(
            part_of(picked.at[y], half), part_of(landed.at[place], half), s4s.at[half, 0]
        ).wait()
        for dx in range(NX):
            for dy in range(NY):
                if dx or dy:
                    j = dx * NY + dy
                    src = lax.rem(x - dx + NX, NX) * NY + lax.rem(y - dy + NY, NY)
                    here = part_of(landed.at[src], half)
                    remote(here, here, s4s.at[half, j], s4r.at[half, j], after).wait_recv()

    def build(s):
        for b in range(9):
            j = s * 9 + b
            lo = (j // 2) * 16
            both = landed[:, lo : lo + 16, :].astype(F32)
            block = both[:, (j % 2) * 8 : (j % 2) * 8 + 8, :].reshape(W, W).astype(BF16)
            amat[s, pl.ds((b // 3) * W, W), pl.ds((b % 3) * W, W)] = block

    sums = []
    for s in range(2):
        landed_half(s)
        build(s)
        if s == 0:
            keep.wait()
        part[s] = jnp.zeros((W, W), F32)
        for i in range(CHUNKS):
            if s == 0:
                part_rows = pl.ds(i * count, count)
                for k, lane in enumerate((0, 2 * W)):
                    here = fcat.at[part_rows, pl.ds(lane, W)]
                    remote(fac.at[part_rows], here, fs.at[k, i], fr.at[k, i], after).wait_recv()

            @pl.loop(0, count // (PSTEP * W))
            def _(q):
                start = pl.multiple_of(i * count + q * PSTEP * W, PSTEP * W)
                block = fcat[pl.ds(start, PSTEP * W), :]
                half = jnp.dot(block, amat[s], preferred_element_type=F32).astype(BF16)
                total = part[s]
                for p in range(PSTEP):
                    total += lax.dot_general(
                        half[p * W : (p + 1) * W],
                        block[p * W : (p + 1) * W],
                        (((1,), (1,)), ((), ())),
                        preferred_element_type=F32,
                    )
                part[s] = total

        for dx in range(1, NX):
            dst = lax.rem(x + dx, NX)
            copy = remote(
                part.at[s, pl.ds(pl.multiple_of(dst * 32, 32), 32)],
                parts.at[s, dx],
                rs.at[s, dx],
                rr.at[s, dx],
                at(dx, 0, 0, 0),
            )
            copy.start()
            sent.append(copy)
    for s in range(2):
        total = part[s, pl.ds(pl.multiple_of(x * 32, 32), 32), :]
        for dx in range(1, NX):
            here = parts.at[s, dx]
            remote(here, here, rs.at[s, dx], rr.at[s, dx], after).wait_recv()
            total += parts[s, dx]
        out[s] = total.astype(BF16)
    for copy in sent:
        copy.wait_send()


def body(factors, amplitudes, left_step, right_step, amp_owner, amp_slot):
    dma, any_space = pltpu.SemaphoreType.DMA, pl.BlockSpec(memory_space=pl.ANY)
    terms = left_step.shape[1]
    return pl.pallas_call(
        kernel,
        out_shape=jax.ShapeDtypeStruct((2, 32, W), BF16),
        in_specs=[any_space] * 6,
        out_specs=pl.BlockSpec(memory_space=pltpu.VMEM),
        scratch_shapes=[
            pltpu.VMEM((2, W, W), BF16),
            pltpu.VMEM((4, 2, terms), jnp.int32),
            pltpu.VMEM((2, 8, W), jnp.int32),
            pltpu.VMEM((NY, 16, W), BF16),
            pltpu.VMEM((NY, 32, 256), BF16),
            pltpu.VMEM((NY, 144, 2048), BF16),
            pltpu.VMEM((256, 2048), BF16),
            pltpu.VMEM((NC, NZ, NY, 16, W), BF16),
            pltpu.VMEM((NY, 144, W), BF16),
            pltpu.VMEM((NX * NY, 144, W), BF16),
            pltpu.VMEM((2, 3 * W, 3 * W), BF16),
            pltpu.VMEM((PAUX * W, 3 * W), BF16),
            pltpu.VMEM((2, W, W), F32),
            pltpu.VMEM((2, NX, 32, W), F32),
            dma((8,)),
            dma((12,)), dma((12,)),
            dma((4,)), dma((4,)),
            dma((15,)), dma((15,)),
            dma((16,)), dma((16,)),
            dma((2, 16)), dma((2, 16)),
            dma((2, CHUNKS)), dma((2, CHUNKS)),
            dma((2, 4)), dma((2, 4)),
        ],
        compiler_params=pltpu.CompilerParams(
            collective_id=0, has_side_effects=True, vmem_limit_bytes=56 * 2**20
        ),
        cost_estimate=pl.CostEstimate(flops=4 * 10**9, bytes_accessed=4 * 2**20, transcendentals=0),
    )(factors.reshape(PAUX * W, W), amplitudes, left_step, right_step, amp_owner, amp_slot)


def solution(mesh):
    return jax.shard_map(
        body,
        mesh=mesh,
        in_specs=(
            P("tile", "fit", None, None),
            P("tile", None, None),
            P("tile", None),
            P("tile", None),
            P("tile", None),
            P("tile", None),
        ),
        out_specs=P("tile", "fit", None),
        check_vma=False,
    )
```

```python
import jax
import jax.numpy as jnp
from jax import lax
from jax.experimental import pallas as pl
from jax.experimental.pallas import tpu as pltpu
from jax.sharding import PartitionSpec as P

NX, NY, NZ, NC = 4, 4, 16, 2
TILES = NY * NZ * NC
W = 128
PAUX = 32
FAR = (0, 5, -5)
NEAR = (1, -1, 2, -2)
CHUNKS = 4
HEAD = 80
EARLY = 1
RELAYED = 2
BF16, F32 = jnp.bfloat16, jnp.float32


def remote(src, dst, send, recv, device):
    return pltpu.make_async_remote_copy(
        src_ref=src,
        dst_ref=dst,
        send_sem=send,
        recv_sem=recv,
        device_id=device,
        device_id_type=pl.DeviceIdType.MESH,
    )


def kernel(
    fac, amp, lstep, rstep, own, slot, out,
    amp_v, idx_v, code, pack, marks, wide, spread, tiles, picked, landed, amat, fcat, part, parts, halves, via,
    loc, s1s, s1r, ms, mr, s2s, s2r, cs, cr, s4s, s4r, fs, fr, rs, rr, vs, vr, ws,
):
    t = lax.axis_index("tile")
    x = lax.axis_index("fit")
    c = lax.rem(t, NC)
    z = lax.rem(t // NC, NZ)
    y = t // (NC * NZ)

    def at(dx, dy, dz, dc):
        yy, zz = lax.rem(y + dy + NY, NY), lax.rem(z + dz + NZ, NZ)
        return ((yy * NZ + zz) * NC + lax.rem(c + dc, NC), lax.rem(x + dx, NX))

    before = (lax.rem(t + TILES - 1, TILES), x)
    after = (lax.rem(t + 1, TILES), x)
    cross = jnp.where(c == 0, before[0], after[0])
    ends = ((z == 0) & (c == 0)) | ((z == NZ - 1) & (c == 1))
    corner = (y * NZ * NC + jnp.where(c == 0, NZ * NC - 1, 0), x)
    direct = (jnp.logical_not(ends & (c == 1)), jnp.logical_not(ends & (c == 0)))

    barrier = pltpu.get_barrier_semaphore()
    peers = []
    for dz in (5, -5, 0):
        for dy in range(NY):
            if dy or dz:
                peers.append(at(0, dy, dz, 0))
    for dz in (1, -1, 2, -2, 3, -3):
        peers.append(at(0, 0, dz, 0))
    peers.append(at(0, 0, 0, 1))
    for dx in range(1, NX):
        for dy in range(NY):
            peers.append(at(dx, dy, 0, 0))
    peers.append((cross, x))
    for peer in peers:
        pl.semaphore_signal(barrier, inc=1, device_id=peer, device_id_type=pl.DeviceIdType.MESH)

    @pl.when(ends)
    def _():
        pl.semaphore_signal(barrier, inc=1, device_id=corner, device_id_type=pl.DeviceIdType.MESH)


    loads = [pltpu.make_async_copy(amp, amp_v, loc.at[0])]
    for i, ref in enumerate((lstep, rstep, own, slot)):
        loads.append(pltpu.make_async_copy(ref, idx_v.at[i], loc.at[1 + i]))
    keep = pltpu.make_async_copy(fac, fcat.at[:, pl.ds(W, W)], loc.at[5])
    for copy in loads:
        copy.start()
    keep.start()

    for copy in loads:
        copy.wait()

    rows = amp_v[:, pl.ds(pl.multiple_of(x * 32, 32), 32), :].astype(F32).reshape(2, NY, 8, W)
    for dest in range(NY):
        pack[dest] = rows[:, dest].reshape(16, W).astype(BF16)

    lpos = jnp.clip(t + idx_v[0], 0, TILES - 1) - t + 1
    rpos = jnp.clip(t + idx_v[1], 0, TILES - 1) - t + 1
    owner = idx_v[2]
    tile = ((((owner & 1) ^ c) * NZ + ((owner >> 1) & (NZ - 1))) * NY + (owner >> 5)) * 2 + idx_v[3]
    terms = lpos.shape[1]
    code[...] = jnp.full(code.shape, -1, jnp.int32)
    code[0, 0:2, 0:terms] = lpos * 3 + rpos
    code[1, 0:2, 0:terms] = tile
    for s in range(2):
        block_of = (lax.broadcasted_iota(jnp.int32, (16, W), 0) == code[0, s : s + 1, :]).astype(BF16)
        tile_of = (lax.broadcasted_iota(jnp.int32, (256, W), 0) == code[1, s : s + 1, :]).astype(BF16)
        both = lax.dot_general(block_of, tile_of, (((1,), (1,)), ((), ())), preferred_element_type=F32)
        marks[y, 16 * s : 16 * (s + 1), :] = both.astype(BF16)
    pl.semaphore_wait(barrier, len(peers) + jnp.where(ends, 1, 0))

    count = PAUX * W // CHUNKS

    def factor_copy(i, k):
        part_rows = pl.ds(i * count, count)
        device, lane = ((after, 0), (before, 2 * W))[k]
        return remote(fac.at[part_rows], fcat.at[part_rows, pl.ds(lane, W)], fs.at[k, i], fr.at[k, i], device)

    def start_factors(lo, hi):
        for i in range(lo, hi):
            for k in range(2):
                copy = factor_copy(i, k)
                if i < RELAYED:
                    copy.start()
                    sent.append(copy)
                else:
                    pl.when(direct[k])(copy.start)

    def relay_copy(i):
        dy = jnp.where(c == 1, 1, -1)
        return remote(
            fac.at[pl.ds(i * count, count)], via.at[i - RELAYED], vs.at[i - RELAYED], vr.at[i - RELAYED], at(0, dy, 0, 0)
        )

    def relay_on(i, k):
        dst = fcat.at[pl.ds(i * count, count), pl.ds(2 * W * k, W)]
        return remote(via.at[i - RELAYED], dst, ws.at[i - RELAYED], fr.at[k, i], corner)

    sent = []
    first = {}
    for dz in (5, -5, 0):
        for dy in range(NY):
            j = FAR.index(dz) * NY + dy
            dst = lax.rem(y + dy, NY)
            if dy or dz:
                first[dz, dy] = remote(pack.at[dst], tiles.at[0, z, y], s1s.at[j], s1r.at[j], at(0, dy, dz, 0))
                first[dz, dy].start()
                sent.append(first[dz, dy])
            else:
                mine = pltpu.make_async_copy(pack.at[dst], tiles.at[0, z, y], loc.at[6])
                mine.start()
    for dy in range(1, NY):
        copy = remote(marks.at[y], marks.at[y], ms.at[dy], mr.at[dy], at(0, dy, 0, 0))
        copy.start()
        sent.append(copy)

    spread[...] = (
        lax.broadcasted_iota(jnp.int32, (256, 2048), 1) // 8 == lax.broadcasted_iota(jnp.int32, (256, 2048), 0)
    ).astype(BF16)

    start_factors(0, EARLY)

    @pl.when(ends)
    def _():
        for i in range(RELAYED, CHUNKS):
            relay_copy(i).start()


    def arrived(dz, dy):
        j = FAR.index(dz) * NY + dy
        zz, yy = lax.rem(z - dz + NZ, NZ), lax.rem(y - dy + NY, NY)
        here = tiles.at[0, zz, yy]
        remote(here, here, s1s.at[j], s1r.at[j], after).wait_recv()

    def tile_block(dz, core=0):
        return tiles.at[core, lax.rem(z - dz + 2 * NZ, NZ)]

    partner = at(0, 0, 0, 1)

    def share(dz):
        j = dz + 7
        copy = remote(tile_block(dz), tile_block(dz, 1), cs.at[j], cr.at[j], partner)
        copy.start()
        sent.append(copy)

    near = []
    for i, dz in enumerate(FAR):
        for dy in range(NY):
            if dy or dz:
                arrived(dz, dy)
        if dz == 0:
            mine.wait()
        steps = NEAR + ((3,) if dz == 5 else ())
        for k, step in enumerate(steps):
            j = i * 5 + k
            copy = remote(tile_block(dz), tile_block(dz), s2s.at[j], s2r.at[j], at(0, 0, step, 0))
            copy.start()
            sent.append(copy)
            near.append((j, dz + step))
        share(dz)

    start_factors(EARLY, CHUNKS)
    for dy in range(1, NY):
        here = marks.at[lax.rem(y - dy + NY, NY)]
        remote(here, here, ms.at[dy], mr.at[dy], after).wait_recv()
    row = lax.broadcasted_iota(jnp.int32, (144, 32), 0) // 8
    col = lax.broadcasted_iota(jnp.int32, (144, 32), 1)
    rowpick = (jnp.where(row >= 9, row + 7, row) == col).astype(BF16)
    same = (lax.broadcasted_iota(jnp.int32, (144, 2048), 0) & 7) == (
        lax.broadcasted_iota(jnp.int32, (144, 2048), 1) & 7
    )
    for dest in range(NY):
        blocks = jnp.dot(rowpick, marks[dest], preferred_element_type=F32).astype(BF16)
        full = jnp.dot(blocks, spread[...], preferred_element_type=F32)
        wide[dest] = jnp.where(same, full, 0.0).astype(BF16)

    for j, dz in near:
        remote(tile_block(dz), tile_block(dz), s2s.at[j], s2r.at[j], after).wait_recv()
        share(dz)

    @pl.when(ends)
    def _():
        for i in range(RELAYED, CHUNKS):
            relay_copy(i).wait_recv()
            for k in range(2):
                pl.when(c == 1 - k)(relay_on(i, k).start)

    own_half = jnp.dot(
        wide[:, :, :1024].reshape(NY * 144, 1024), tiles[0].reshape(1024, W), preferred_element_type=F32
    )
    for dz in range(-7, 9):
        here = tile_block(dz, 1)
        remote(here, here, cs.at[dz + 7], cr.at[dz + 7], after).wait_recv()
    other_half = jnp.dot(
        wide[:, :, 1024:].reshape(NY * 144, 1024), tiles[1].reshape(1024, W), preferred_element_type=F32
    )
    picked[...] = (own_half + other_half).astype(BF16).reshape(NY, 144, W)

    place = x * NY + y

    def half_of(ref, s):
        return ref.at[pl.ds(0, HEAD)] if s == 0 else ref.at[pl.ds(HEAD, 144 - HEAD)]

    kept = []
    for s in range(2):
        for dx in range(NX):
            for dy in range(NY):
                src_ref, dst_ref = half_of(picked.at[lax.rem(y + dy, NY)], s), half_of(landed.at[place], s)
                j = dx * NY + dy
                if dx or dy:
                    copy = remote(src_ref, dst_ref, s4s.at[s, j], s4r.at[s, j], at(dx, dy, 0, 0))
                    sent.append(copy)
                else:
                    copy = pltpu.make_async_copy(src_ref, dst_ref, s4s.at[s, 0])
                    kept.append(copy)
                copy.start()

    def blocks_here(s):
        kept[s].wait()
        for dx in range(NX):
            for dy in range(NY):
                if dx or dy:
                    j = dx * NY + dy
                    here = half_of(landed.at[lax.rem(x - dx + NX, NX) * NY + lax.rem(y - dy + NY, NY)], s)
                    remote(here, here, s4s.at[s, j], s4r.at[s, j], after).wait_recv()
        for b in range(9):
            j = s * 9 + b
            both = landed[:, (j // 2) * 16 : (j // 2) * 16 + 16, :].astype(F32)
            block = both[:, (j % 2) * 8 : (j % 2) * 8 + 8, :].reshape(W, W).astype(BF16)
            amat[s, pl.ds((b // 3) * W, W), pl.ds((b % 3) * W, W)] = block

    def factors_here(i):
        for k, lane in enumerate((0, 2 * W)):
            here = fcat.at[pl.ds(i * count, count), pl.ds(lane, W)]
            remote(fac.at[pl.ds(i * count, count)], here, fs.at[k, i], fr.at[k, i], after).wait_recv()

    def right_products(i, s):
        halves[i % 2] = jnp.dot(fcat[pl.ds(i * count, count), :], amat[s], preferred_element_type=F32).astype(BF16)

    def left_products(i, s):
        half, block = halves[i % 2], fcat[pl.ds(i * count, count), :]
        steps = range(0, count, W)
        right = jnp.concatenate([block[p : p + W] for p in steps], axis=1)
        left = jnp.concatenate([half[p : p + W] for p in steps], axis=1)
        term = lax.dot_general(left, right, (((1,), (1,)), ((), ())), preferred_element_type=F32)
        part[s] = term if i == 0 else part[s] + term

    def reduce_start(s):
        for dx in range(1, NX):
            rows = pl.ds(pl.multiple_of(lax.rem(x + dx, NX) * 32, 32), 32)
            copy = remote(part.at[s, rows], parts.at[dx, s], rs.at[s, dx], rr.at[s, dx], at(dx, 0, 0, 0))
            copy.start()
            sent.append(copy)

    keep.wait()
    for s in range(2):
        blocks_here(s)
        for i in range(CHUNKS):
            if s == 0:
                factors_here(i)
            right_products(i, s)
            if i:
                left_products(i - 1, s)
        left_products(CHUNKS - 1, s)
        reduce_start(s)
    total = part[:, pl.ds(pl.multiple_of(x * 32, 32), 32), :]
    for dx in range(1, NX):
        for s in range(2):
            here = parts.at[dx, s]
            remote(here, here, rs.at[s, dx], rr.at[s, dx], after).wait_recv()
        total += parts[dx]
    out[...] = total.astype(BF16)
    for copy in sent:
        copy.wait_send()
    for i in range(RELAYED, CHUNKS):
        for k in range(2):
            pl.when(direct[k])(factor_copy(i, k).wait_send)

    @pl.when(ends)
    def _():
        for i in range(RELAYED, CHUNKS):
            relay_copy(i).wait_send()
            relay_on(i, 0).wait_send()


def body(factors, amplitudes, left_step, right_step, amp_owner, amp_slot):
    dma, any_space = pltpu.SemaphoreType.DMA, pl.BlockSpec(memory_space=pl.ANY)
    terms = left_step.shape[1]
    return pl.pallas_call(
        kernel,
        out_shape=jax.ShapeDtypeStruct((2, 32, W), BF16),
        in_specs=[any_space] * 6,
        out_specs=pl.BlockSpec(memory_space=pltpu.VMEM),
        scratch_shapes=[
            pltpu.VMEM((2, W, W), BF16),
            pltpu.VMEM((4, 2, terms), jnp.int32),
            pltpu.VMEM((2, 8, W), jnp.int32),
            pltpu.VMEM((NY, 16, W), BF16),
            pltpu.VMEM((NY, 32, 256), BF16),
            pltpu.VMEM((NY, 144, 2048), BF16),
            pltpu.VMEM((256, 2048), BF16),
            pltpu.VMEM((NC, NZ, NY, 16, W), BF16),
            pltpu.VMEM((NY, 144, W), BF16),
            pltpu.VMEM((NX * NY, 144, W), BF16),
            pltpu.VMEM((2, 3 * W, 3 * W), BF16),
            pltpu.VMEM((PAUX * W, 3 * W), BF16),
            pltpu.VMEM((2, W, W), F32),
            pltpu.VMEM((NX, 2, 32, W), F32),
            pltpu.VMEM((2, PAUX * W // CHUNKS, 3 * W), BF16),
            pltpu.VMEM((CHUNKS - RELAYED, PAUX * W // CHUNKS, W), BF16),
            dma((8,)),
            dma((12,)), dma((12,)),
            dma((4,)), dma((4,)),
            dma((15,)), dma((15,)),
            dma((16,)), dma((16,)),
            dma((2, 16)), dma((2, 16)),
            dma((2, CHUNKS)), dma((2, CHUNKS)),
            dma((2, 4)), dma((2, 4)),
            dma((CHUNKS - RELAYED,)), dma((CHUNKS - RELAYED,)), dma((CHUNKS - RELAYED,)),
        ],
        compiler_params=pltpu.CompilerParams(
            collective_id=0, has_side_effects=True, vmem_limit_bytes=56 * 2**20
        ),
        cost_estimate=pl.CostEstimate(flops=4 * 10**9, bytes_accessed=4 * 2**20, transcendentals=0),
    )(factors.reshape(PAUX * W, W), amplitudes, left_step, right_step, amp_owner, amp_slot)


def solution(mesh):
    return jax.shard_map(
        body,
        mesh=mesh,
        in_specs=(
            P("tile", "fit", None, None),
            P("tile", None, None),
            P("tile", None),
            P("tile", None),
            P("tile", None),
            P("tile", None),
        ),
        out_specs=P("tile", "fit", None),
        check_vma=False,
    )
```

```python
import jax
import jax.numpy as jnp
from jax import lax
from jax.experimental import pallas as pl
from jax.experimental.pallas import tpu as pltpu
from jax.sharding import PartitionSpec as P

NX, NY, NZ, NC = 4, 4, 16, 2
TILES = NY * NZ * NC
W = 128
PAUX = 32
FAR = (0, 5, -5)
NEAR = (1, -1, 2, -2)
CHUNKS = 4
GROUP = 48
ORDER = (1, 0, 2)
EARLY = 1
RELAYED = 2
BF16, F32 = jnp.bfloat16, jnp.float32


def remote(src, dst, send, recv, device):
    return pltpu.make_async_remote_copy(
        src_ref=src,
        dst_ref=dst,
        send_sem=send,
        recv_sem=recv,
        device_id=device,
        device_id_type=pl.DeviceIdType.MESH,
    )


def kernel(
    fac, amp, lstep, rstep, own, slot, out,
    amp_v, idx_v, code, pack, marks, wide, spread, tiles, picked, landed, amat, fcat, part, parts, halves, via,
    loc, s1s, s1r, ms, mr, s2s, s2r, cs, cr, s4s, s4r, fs, fr, rs, rr, vs, vr, ws,
):
    t = lax.axis_index("tile")
    x = lax.axis_index("fit")
    c = lax.rem(t, NC)
    z = lax.rem(t // NC, NZ)
    y = t // (NC * NZ)

    def at(dx, dy, dz, dc):
        yy, zz = lax.rem(y + dy + NY, NY), lax.rem(z + dz + NZ, NZ)
        return ((yy * NZ + zz) * NC + lax.rem(c + dc, NC), lax.rem(x + dx, NX))

    before = (lax.rem(t + TILES - 1, TILES), x)
    after = (lax.rem(t + 1, TILES), x)
    cross = jnp.where(c == 0, before[0], after[0])
    ends = ((z == 0) & (c == 0)) | ((z == NZ - 1) & (c == 1))
    corner = (y * NZ * NC + jnp.where(c == 0, NZ * NC - 1, 0), x)
    direct = (jnp.logical_not(ends & (c == 1)), jnp.logical_not(ends & (c == 0)))

    barrier = pltpu.get_barrier_semaphore()
    peers = []
    for dz in (5, -5, 0):
        for dy in range(NY):
            if dy or dz:
                peers.append(at(0, dy, dz, 0))
    for dz in (1, -1, 2, -2, 3, -3):
        peers.append(at(0, 0, dz, 0))
    peers.append(at(0, 0, 0, 1))
    for dx in range(1, NX):
        for dy in range(NY):
            peers.append(at(dx, dy, 0, 0))
    peers.append((cross, x))
    for peer in peers:
        pl.semaphore_signal(barrier, inc=1, device_id=peer, device_id_type=pl.DeviceIdType.MESH)

    @pl.when(ends)
    def _():
        pl.semaphore_signal(barrier, inc=1, device_id=corner, device_id_type=pl.DeviceIdType.MESH)


    loads = [pltpu.make_async_copy(amp, amp_v, loc.at[0])]
    for i, ref in enumerate((lstep, rstep, own, slot)):
        loads.append(pltpu.make_async_copy(ref, idx_v.at[i], loc.at[1 + i]))
    keep = pltpu.make_async_copy(fac, fcat.at[:, pl.ds(W, W)], loc.at[5])
    for copy in loads:
        copy.start()
    keep.start()

    for copy in loads:
        copy.wait()

    rows = amp_v[:, pl.ds(pl.multiple_of(x * 32, 32), 32), :].astype(F32).reshape(2, NY, 8, W)
    for dest in range(NY):
        pack[dest] = rows[:, dest].reshape(16, W).astype(BF16)

    lpos = jnp.clip(t + idx_v[0], 0, TILES - 1) - t + 1
    rpos = jnp.clip(t + idx_v[1], 0, TILES - 1) - t + 1
    owner = idx_v[2]
    tile = ((((owner & 1) ^ c) * NZ + ((owner >> 1) & (NZ - 1))) * NY + (owner >> 5)) * 2 + idx_v[3]
    terms = lpos.shape[1]
    code[...] = jnp.full(code.shape, -1, jnp.int32)
    code[0, 0:2, 0:terms] = lpos * 3 + rpos
    code[1, 0:2, 0:terms] = tile
    for s in range(2):
        block_of = (lax.broadcasted_iota(jnp.int32, (16, W), 0) == code[0, s : s + 1, :]).astype(BF16)
        tile_of = (lax.broadcasted_iota(jnp.int32, (256, W), 0) == code[1, s : s + 1, :]).astype(BF16)
        both = lax.dot_general(block_of, tile_of, (((1,), (1,)), ((), ())), preferred_element_type=F32)
        marks[y, 16 * s : 16 * (s + 1), :] = both.astype(BF16)
    pl.semaphore_wait(barrier, len(peers) + jnp.where(ends, 1, 0))

    count = PAUX * W // CHUNKS

    def factor_copy(i, k):
        part_rows = pl.ds(i * count, count)
        device, lane = ((after, 0), (before, 2 * W))[k]
        return remote(fac.at[part_rows], fcat.at[part_rows, pl.ds(lane, W)], fs.at[k, i], fr.at[k, i], device)

    def start_factors(lo, hi):
        for i in range(lo, hi):
            for k in range(2):
                copy = factor_copy(i, k)
                if i < RELAYED:
                    copy.start()
                    sent.append(copy)
                else:
                    pl.when(direct[k])(copy.start)

    def relay_copy(i):
        dy = jnp.where(c == 1, 1, -1)
        return remote(
            fac.at[pl.ds(i * count, count)], via.at[i - RELAYED], vs.at[i - RELAYED], vr.at[i - RELAYED], at(0, dy, 0, 0)
        )

    def relay_on(i, k):
        dst = fcat.at[pl.ds(i * count, count), pl.ds(2 * W * k, W)]
        return remote(via.at[i - RELAYED], dst, ws.at[i - RELAYED], fr.at[k, i], corner)

    sent = []
    first = {}
    for dz in (5, -5, 0):
        for dy in range(NY):
            j = FAR.index(dz) * NY + dy
            dst = lax.rem(y + dy, NY)
            if dy or dz:
                first[dz, dy] = remote(pack.at[dst], tiles.at[0, z, y], s1s.at[j], s1r.at[j], at(0, dy, dz, 0))
                first[dz, dy].start()
                sent.append(first[dz, dy])
            else:
                mine = pltpu.make_async_copy(pack.at[dst], tiles.at[0, z, y], loc.at[6])
                mine.start()
    for dy in range(1, NY):
        copy = remote(marks.at[y], marks.at[y], ms.at[dy], mr.at[dy], at(0, dy, 0, 0))
        copy.start()
        sent.append(copy)

    spread[...] = (
        lax.broadcasted_iota(jnp.int32, (256, 2048), 1) // 8 == lax.broadcasted_iota(jnp.int32, (256, 2048), 0)
    ).astype(BF16)

    start_factors(0, EARLY)

    @pl.when(ends)
    def _():
        for i in range(RELAYED, CHUNKS):
            relay_copy(i).start()


    def arrived(dz, dy):
        j = FAR.index(dz) * NY + dy
        zz, yy = lax.rem(z - dz + NZ, NZ), lax.rem(y - dy + NY, NY)
        here = tiles.at[0, zz, yy]
        remote(here, here, s1s.at[j], s1r.at[j], after).wait_recv()

    def tile_block(dz, core=0):
        return tiles.at[core, lax.rem(z - dz + 2 * NZ, NZ)]

    partner = at(0, 0, 0, 1)

    def share(dz):
        j = dz + 7
        copy = remote(tile_block(dz), tile_block(dz, 1), cs.at[j], cr.at[j], partner)
        copy.start()
        sent.append(copy)

    near = []
    for i, dz in enumerate(FAR):
        for dy in range(NY):
            if dy or dz:
                arrived(dz, dy)
        if dz == 0:
            mine.wait()
        steps = NEAR + ((3,) if dz == 5 else ())
        for k, step in enumerate(steps):
            j = i * 5 + k
            copy = remote(tile_block(dz), tile_block(dz), s2s.at[j], s2r.at[j], at(0, 0, step, 0))
            copy.start()
            sent.append(copy)
            near.append((j, dz + step))
        share(dz)

    start_factors(EARLY, CHUNKS)
    for dy in range(1, NY):
        here = marks.at[lax.rem(y - dy + NY, NY)]
        remote(here, here, ms.at[dy], mr.at[dy], after).wait_recv()
    row = lax.broadcasted_iota(jnp.int32, (144, 32), 0) // 8
    col = lax.broadcasted_iota(jnp.int32, (144, 32), 1)
    rowpick = (row // 6 + 3 * (row % 3) + 16 * ((row // 3) & 1) == col).astype(BF16)
    same = (lax.broadcasted_iota(jnp.int32, (144, 2048), 0) & 7) == (
        lax.broadcasted_iota(jnp.int32, (144, 2048), 1) & 7
    )
    for dest in range(NY):
        blocks = jnp.dot(rowpick, marks[dest], preferred_element_type=F32).astype(BF16)
        full = jnp.dot(blocks, spread[...], preferred_element_type=F32)
        wide[dest] = jnp.where(same, full, 0.0).astype(BF16)

    for j, dz in near:
        remote(tile_block(dz), tile_block(dz), s2s.at[j], s2r.at[j], after).wait_recv()
        share(dz)

    @pl.when(ends)
    def _():
        for i in range(RELAYED, CHUNKS):
            relay_copy(i).wait_recv()
            for k in range(2):
                pl.when(c == 1 - k)(relay_on(i, k).start)

    def picks(g, core):
        marked = wide[:, GROUP * g : GROUP * (g + 1), 1024 * core : 1024 * (core + 1)].reshape(NY * GROUP, 1024)
        return jnp.dot(marked, tiles[core].reshape(1024, W), preferred_element_type=F32)

    own_half = [picks(g, 0) for g in ORDER]
    for dz in range(-7, 9):
        here = tile_block(dz, 1)
        remote(here, here, cs.at[dz + 7], cr.at[dz + 7], after).wait_recv()
    place = x * NY + y

    def group_of(ref, g):
        return ref.at[pl.ds(GROUP * g, GROUP)]

    kept = {}
    for n, g in enumerate(ORDER):
        both = (own_half[n] + picks(g, 1)).astype(BF16)
        picked[:, GROUP * g : GROUP * (g + 1), :] = both.reshape(NY, GROUP, W)
        for dx in (2, 1, 3, 0):
            for dy in (2, 1, 3, 0):
                src_ref, dst_ref = group_of(picked.at[lax.rem(y + dy, NY)], g), group_of(landed.at[place], g)
                j = dx * NY + dy
                if dx or dy:
                    copy = remote(src_ref, dst_ref, s4s.at[g, j], s4r.at[g, j], at(dx, dy, 0, 0))
                    sent.append(copy)
                else:
                    copy = kept[g] = pltpu.make_async_copy(src_ref, dst_ref, s4s.at[g, 0])
                copy.start()

    def blocks_here(g):
        kept[g].wait()
        for dx in range(NX):
            for dy in range(NY):
                if dx or dy:
                    j = dx * NY + dy
                    here = group_of(landed.at[lax.rem(x - dx + NX, NX) * NY + lax.rem(y - dy + NY, NY)], g)
                    remote(here, here, s4s.at[g, j], s4r.at[g, j], after).wait_recv()
        for j in range(0, 6, 2):
            lo = GROUP * g + 8 * j
            both = landed[:, lo : lo + 16, :].astype(F32)
            for k in range(2):
                s, left = divmod(j + k, 3)
                block = both[:, 8 * k : 8 * k + 8, :].reshape(W, W).astype(BF16)
                amat[g, pl.ds(left * W, W), pl.ds(s * W, W)] = block

    def factors_here(i):
        for k, lane in enumerate((0, 2 * W)):
            here = fcat.at[pl.ds(i * count, count), pl.ds(lane, W)]
            remote(fac.at[pl.ds(i * count, count)], here, fs.at[k, i], fr.at[k, i], after).wait_recv()

    def right_products(i, g):
        halves[i % 2] = jnp.dot(fcat[pl.ds(i * count, count), :], amat[g], preferred_element_type=F32).astype(BF16)

    def left_products(i, g):
        half, block = halves[i % 2], fcat[pl.ds(i * count, count), g * W : (g + 1) * W]
        steps = range(0, count, W)
        right = jnp.concatenate([block[p : p + W] for p in steps], axis=1)
        left = jnp.concatenate(
            [jnp.concatenate([half[p : p + W, s * W : (s + 1) * W] for p in steps], axis=1) for s in range(2)], axis=0
        )
        term = lax.dot_general(left, right, (((1,), (1,)), ((), ())), preferred_element_type=F32)
        part[...] += term.reshape(2, W, W)

    keep.wait()
    part[...] = jnp.zeros(part.shape, F32)
    todo = [(i, g) for g in ORDER for i in range(CHUNKS)]
    for n, (i, g) in enumerate(todo):
        if i == 0:
            blocks_here(g)
        if g == ORDER[0]:
            factors_here(i)
        right_products(i, g)
        if n:
            left_products(*todo[n - 1])
    left_products(*todo[-1])

    for dx in (2, 1, 3):
        rows = pl.ds(pl.multiple_of(lax.rem(x + dx, NX) * 32, 32), 32)
        copy = remote(part.at[:, rows], parts.at[dx], rs.at[dx], rr.at[dx], at(dx, 0, 0, 0))
        copy.start()
        sent.append(copy)
    total = part[:, pl.ds(pl.multiple_of(x * 32, 32), 32), :]
    for dx in range(1, NX):
        here = parts.at[dx]
        remote(here, here, rs.at[dx], rr.at[dx], after).wait_recv()
        total += parts[dx]
    out[...] = total.astype(BF16)
    for copy in sent:
        copy.wait_send()
    for i in range(RELAYED, CHUNKS):
        for k in range(2):
            pl.when(direct[k])(factor_copy(i, k).wait_send)

    @pl.when(ends)
    def _():
        for i in range(RELAYED, CHUNKS):
            relay_copy(i).wait_send()
            relay_on(i, 0).wait_send()


def body(factors, amplitudes, left_step, right_step, amp_owner, amp_slot):
    dma, any_space = pltpu.SemaphoreType.DMA, pl.BlockSpec(memory_space=pl.ANY)
    terms = left_step.shape[1]
    return pl.pallas_call(
        kernel,
        out_shape=jax.ShapeDtypeStruct((2, 32, W), BF16),
        in_specs=[any_space] * 6,
        out_specs=pl.BlockSpec(memory_space=pltpu.VMEM),
        scratch_shapes=[
            pltpu.VMEM((2, W, W), BF16),
            pltpu.VMEM((4, 2, terms), jnp.int32),
            pltpu.VMEM((2, 8, W), jnp.int32),
            pltpu.VMEM((NY, 16, W), BF16),
            pltpu.VMEM((NY, 32, 256), BF16),
            pltpu.VMEM((NY, 144, 2048), BF16),
            pltpu.VMEM((256, 2048), BF16),
            pltpu.VMEM((NC, NZ, NY, 16, W), BF16),
            pltpu.VMEM((NY, 144, W), BF16),
            pltpu.VMEM((NX * NY, 144, W), BF16),
            pltpu.VMEM((3, 3 * W, 2 * W), BF16),
            pltpu.VMEM((PAUX * W, 3 * W), BF16),
            pltpu.VMEM((2, W, W), F32),
            pltpu.VMEM((NX, 2, 32, W), F32),
            pltpu.VMEM((2, PAUX * W // CHUNKS, 2 * W), BF16),
            pltpu.VMEM((CHUNKS - RELAYED, PAUX * W // CHUNKS, W), BF16),
            dma((8,)),
            dma((12,)), dma((12,)),
            dma((4,)), dma((4,)),
            dma((15,)), dma((15,)),
            dma((16,)), dma((16,)),
            dma((3, 16)), dma((3, 16)),
            dma((2, CHUNKS)), dma((2, CHUNKS)),
            dma((4,)), dma((4,)),
            dma((CHUNKS - RELAYED,)), dma((CHUNKS - RELAYED,)), dma((CHUNKS - RELAYED,)),
        ],
        compiler_params=pltpu.CompilerParams(
            collective_id=0, has_side_effects=True, vmem_limit_bytes=56 * 2**20
        ),
        cost_estimate=pl.CostEstimate(flops=4 * 10**9, bytes_accessed=4 * 2**20, transcendentals=0),
    )(factors.reshape(PAUX * W, W), amplitudes, left_step, right_step, amp_owner, amp_slot)


def solution(mesh):
    return jax.shard_map(
        body,
        mesh=mesh,
        in_specs=(
            P("tile", "fit", None, None),
            P("tile", None, None),
            P("tile", None),
            P("tile", None),
            P("tile", None),
            P("tile", None),
        ),
        out_specs=P("tile", "fit", None),
        check_vma=False,
    )
```

```python
import jax
import jax.numpy as jnp
from jax import lax
from jax.experimental import pallas as pl
from jax.experimental.pallas import tpu as pltpu
from jax.sharding import PartitionSpec as P

NX, NY, NZ, NC = 4, 4, 16, 2
TILES = NY * NZ * NC
W = 128
PAUX = 32
FAR = (0, 5, -5)
NEAR = (1, -1, 2, -2)
CHUNKS = 4
GROUP = 48
ORDER = (1, 0, 2)
EARLY = 1
RELAYED = 2
BF16, F32 = jnp.bfloat16, jnp.float32


def remote(src, dst, send, recv, device):
    return pltpu.make_async_remote_copy(
        src_ref=src,
        dst_ref=dst,
        send_sem=send,
        recv_sem=recv,
        device_id=device,
        device_id_type=pl.DeviceIdType.MESH,
    )


def kernel(
    fac, amp, lstep, rstep, own, slot, out,
    amp_v, idx_v, code, pack, marks, wide, spread, tiles, picked, landed, amat, fcat, part, parts, halves, via,
    loc, s1s, s1r, ms, mr, s2s, s2r, cs, cr, s4s, s4r, fs, fr, rs, rr, vs, vr, ws,
):
    t = lax.axis_index("tile")
    x = lax.axis_index("fit")
    c = lax.rem(t, NC)
    z = lax.rem(t // NC, NZ)
    y = t // (NC * NZ)

    def at(dx, dy, dz, dc):
        yy, zz = lax.rem(y + dy + NY, NY), lax.rem(z + dz + NZ, NZ)
        return ((yy * NZ + zz) * NC + lax.rem(c + dc, NC), lax.rem(x + dx, NX))

    before = (lax.rem(t + TILES - 1, TILES), x)
    after = (lax.rem(t + 1, TILES), x)
    cross = jnp.where(c == 0, before[0], after[0])
    ends = ((z == 0) & (c == 0)) | ((z == NZ - 1) & (c == 1))
    corner = (y * NZ * NC + jnp.where(c == 0, NZ * NC - 1, 0), x)
    direct = (jnp.logical_not(ends & (c == 1)), jnp.logical_not(ends & (c == 0)))

    barrier = pltpu.get_barrier_semaphore()
    steps = {(0, 0, 0, 1)}
    for dy in range(NY):
        steps |= {(0, dy, dz, 0) for dz in FAR} | {(dx, dy, 0, 0) for dx in range(NX)}
    steps |= {(0, 0, dz, 0) for dz in (1, -1, 2, -2, 3, -3)}
    steps.discard((0, 0, 0, 0))

    def hops(step):
        return (min(step[0], NX - step[0]) + min(step[1], NY - step[1]) + abs(step[2]), step)

    peers = [at(*step) for step in sorted(steps, key=hops, reverse=True)]
    peers.append((cross, x))
    for peer in peers:
        pl.semaphore_signal(barrier, inc=1, device_id=peer, device_id_type=pl.DeviceIdType.MESH)

    @pl.when(ends)
    def _():
        pl.semaphore_signal(barrier, inc=1, device_id=corner, device_id_type=pl.DeviceIdType.MESH)


    loads = [pltpu.make_async_copy(amp, amp_v, loc.at[0])]
    for i, ref in enumerate((lstep, rstep, own, slot)):
        loads.append(pltpu.make_async_copy(ref, idx_v.at[i], loc.at[1 + i]))
    keep = pltpu.make_async_copy(fac, fcat.at[:, pl.ds(W, W)], loc.at[5])
    for copy in loads:
        copy.start()
    keep.start()

    for copy in loads:
        copy.wait()

    rows = amp_v[:, pl.ds(pl.multiple_of(x * 32, 32), 32), :].astype(F32).reshape(2, NY, 8, W)
    for dest in range(NY):
        pack[dest] = rows[:, dest].reshape(16, W).astype(BF16)

    lpos = jnp.clip(t + idx_v[0], 0, TILES - 1) - t + 1
    rpos = jnp.clip(t + idx_v[1], 0, TILES - 1) - t + 1
    owner = idx_v[2]
    tile = ((((owner & 1) ^ c) * NZ + ((owner >> 1) & (NZ - 1))) * NY + (owner >> 5)) * 2 + idx_v[3]
    terms = lpos.shape[1]
    code[...] = jnp.full(code.shape, -1, jnp.int32)
    code[0, 0:2, 0:terms] = lpos * 3 + rpos
    code[1, 0:2, 0:terms] = tile
    for s in range(2):
        block_of = (lax.broadcasted_iota(jnp.int32, (16, W), 0) == code[0, s : s + 1, :]).astype(BF16)
        tile_of = (lax.broadcasted_iota(jnp.int32, (256, W), 0) == code[1, s : s + 1, :]).astype(BF16)
        both = lax.dot_general(block_of, tile_of, (((1,), (1,)), ((), ())), preferred_element_type=F32)
        marks[y, 16 * s : 16 * (s + 1), :] = both.astype(BF16)
    pl.semaphore_wait(barrier, len(peers) + jnp.where(ends, 1, 0))

    count = PAUX * W // CHUNKS

    def factor_copy(i, k):
        part_rows = pl.ds(i * count, count)
        device, lane = ((after, 0), (before, 2 * W))[k]
        return remote(fac.at[part_rows], fcat.at[part_rows, pl.ds(lane, W)], fs.at[k, i], fr.at[k, i], device)

    def start_factors(lo, hi):
        for i in range(lo, hi):
            for k in range(2):
                copy = factor_copy(i, k)
                if i < RELAYED:
                    copy.start()
                    sent.append(copy)
                else:
                    pl.when(direct[k])(copy.start)

    def relay_copy(i):
        dy = jnp.where(c == 1, 1, -1)
        return remote(
            fac.at[pl.ds(i * count, count)], via.at[i - RELAYED], vs.at[i - RELAYED], vr.at[i - RELAYED], at(0, dy, 0, 0)
        )

    def relay_on(i, k):
        dst = fcat.at[pl.ds(i * count, count), pl.ds(2 * W * k, W)]
        return remote(via.at[i - RELAYED], dst, ws.at[i - RELAYED], fr.at[k, i], corner)

    sent = []
    first = {}
    for dz in (5, -5, 0):
        for dy in (2, 1, 3, 0):
            j = FAR.index(dz) * NY + dy
            dst = lax.rem(y + dy, NY)
            if dy or dz:
                first[dz, dy] = remote(pack.at[dst], tiles.at[0, z, y], s1s.at[j], s1r.at[j], at(0, dy, dz, 0))
                first[dz, dy].start()
                sent.append(first[dz, dy])
            else:
                mine = pltpu.make_async_copy(pack.at[dst], tiles.at[0, z, y], loc.at[6])
                mine.start()
    for dy in range(1, NY):
        copy = remote(marks.at[y], marks.at[y], ms.at[dy], mr.at[dy], at(0, dy, 0, 0))
        copy.start()
        sent.append(copy)

    spread[...] = (
        lax.broadcasted_iota(jnp.int32, (256, 2048), 1) // 8 == lax.broadcasted_iota(jnp.int32, (256, 2048), 0)
    ).astype(BF16)

    start_factors(0, EARLY)

    @pl.when(ends)
    def _():
        for i in range(RELAYED, CHUNKS):
            relay_copy(i).start()


    def arrived(dz, dy):
        j = FAR.index(dz) * NY + dy
        zz, yy = lax.rem(z - dz + NZ, NZ), lax.rem(y - dy + NY, NY)
        here = tiles.at[0, zz, yy]
        remote(here, here, s1s.at[j], s1r.at[j], after).wait_recv()

    def tile_block(dz, core=0):
        return tiles.at[core, lax.rem(z - dz + 2 * NZ, NZ)]

    partner = at(0, 0, 0, 1)

    def share(dz):
        j = dz + 7
        copy = remote(tile_block(dz), tile_block(dz, 1), cs.at[j], cr.at[0], partner)
        copy.start()
        sent.append(copy)

    near = []
    for i, dz in enumerate(FAR):
        for dy in range(NY):
            if dy or dz:
                arrived(dz, dy)
        if dz == 0:
            mine.wait()
        steps = NEAR + ((3,) if dz == 5 else ())
        for k, step in enumerate(steps):
            j = i * 5 + k
            copy = remote(tile_block(dz), tile_block(dz), s2s.at[j], s2r.at[j], at(0, 0, step, 0))
            copy.start()
            sent.append(copy)
            near.append((j, dz + step))
        share(dz)

    start_factors(EARLY, CHUNKS)
    for dy in range(1, NY):
        here = marks.at[lax.rem(y - dy + NY, NY)]
        remote(here, here, ms.at[dy], mr.at[dy], after).wait_recv()
    row = lax.broadcasted_iota(jnp.int32, (144, 32), 0) // 8
    col = lax.broadcasted_iota(jnp.int32, (144, 32), 1)
    rowpick = (row // 6 + 3 * (row % 3) + 16 * ((row // 3) & 1) == col).astype(BF16)
    same = (lax.broadcasted_iota(jnp.int32, (144, 2048), 0) & 7) == (
        lax.broadcasted_iota(jnp.int32, (144, 2048), 1) & 7
    )
    for dest in range(NY):
        blocks = jnp.dot(rowpick, marks[dest], preferred_element_type=F32).astype(BF16)
        full = jnp.dot(blocks, spread[...], preferred_element_type=F32)
        wide[dest] = jnp.where(same, full, 0.0).astype(BF16)

    for j, dz in near:
        remote(tile_block(dz), tile_block(dz), s2s.at[j], s2r.at[j], after).wait_recv()
        share(dz)

    @pl.when(ends)
    def _():
        for i in range(RELAYED, CHUNKS):
            relay_copy(i).wait_recv()
            for k in range(2):
                pl.when(c == 1 - k)(relay_on(i, k).start)

    def picks(g, core):
        marked = wide[:, GROUP * g : GROUP * (g + 1), 1024 * core : 1024 * (core + 1)].reshape(NY * GROUP, 1024)
        return jnp.dot(marked, tiles[core].reshape(1024, W), preferred_element_type=F32)

    own_half = [picks(g, 0) for g in ORDER]
    remote(tiles.at[1], tiles.at[1], cs.at[0], cr.at[0], partner).wait_recv()

    place = x * NY + y

    def group_of(ref, g):
        return ref.at[pl.ds(GROUP * g, GROUP)]

    kept = {}
    for n, g in enumerate(ORDER):
        both = (own_half[n] + picks(g, 1)).astype(BF16)
        picked[:, GROUP * g : GROUP * (g + 1), :] = both.reshape(NY, GROUP, W)
        for dx in (2, 1, 3, 0):
            for dy in (2, 1, 3, 0):
                src_ref, dst_ref = group_of(picked.at[lax.rem(y + dy, NY)], g), group_of(landed.at[place], g)
                j = dx * NY + dy
                if dx or dy:
                    copy = remote(src_ref, dst_ref, s4s.at[g, j], s4r.at[g], at(dx, dy, 0, 0))
                    sent.append(copy)
                else:
                    copy = kept[g] = pltpu.make_async_copy(src_ref, dst_ref, s4s.at[g, 0])
                copy.start()

    def blocks_here(g):
        kept[g].wait()
        others = landed.at[pl.ds(0, NX * NY - 1), pl.ds(GROUP * g, GROUP)]
        remote(others, others, s4s.at[g, 1], s4r.at[g], after).wait_recv()
        for j in range(0, 6, 2):
            lo = GROUP * g + 8 * j
            both = landed[:, lo : lo + 16, :].astype(F32)
            for k in range(2):
                s, left = divmod(j + k, 3)
                block = both[:, 8 * k : 8 * k + 8, :].reshape(W, W).astype(BF16)
                amat[g, pl.ds(left * W, W), pl.ds(s * W, W)] = block

    def factors_here(i):
        for k, lane in enumerate((0, 2 * W)):
            here = fcat.at[pl.ds(i * count, count), pl.ds(lane, W)]
            remote(fac.at[pl.ds(i * count, count)], here, fs.at[k, i], fr.at[k, i], after).wait_recv()

    def right_products(i, g):
        halves[i % 2] = jnp.dot(fcat[pl.ds(i * count, count), :], amat[g], preferred_element_type=F32).astype(BF16)

    def left_products(i, g):
        half, block = halves[i % 2], fcat[pl.ds(i * count, count), g * W : (g + 1) * W]
        steps = range(0, count, W)
        right = jnp.concatenate([block[p : p + W] for p in steps], axis=1)
        for s in range(2):
            left = jnp.concatenate([half[p : p + W, s * W : (s + 1) * W] for p in steps], axis=1)
            part[s] += lax.dot_general(left, right, (((1,), (1,)), ((), ())), preferred_element_type=F32)

    keep.wait()
    part[...] = jnp.zeros(part.shape, F32)
    todo = [(i, g) for g in ORDER for i in range(CHUNKS)]
    for n, (i, g) in enumerate(todo):
        if i == 0:
            blocks_here(g)
        if g == ORDER[0]:
            factors_here(i)
        right_products(i, g)
        if n:
            left_products(*todo[n - 1])
    left_products(*todo[-1])

    last = []
    for dx in (2, 1, 3):
        rows = pl.ds(pl.multiple_of(lax.rem(x + dx, NX) * 32, 32), 32)
        copy = remote(part.at[:, rows], parts.at[dx], rs.at[dx], rr.at[dx], at(dx, 0, 0, 0))
        copy.start()
        last.append(copy)
    for copy in sent:
        copy.wait_send()
    for i in range(RELAYED, CHUNKS):
        for k in range(2):
            pl.when(direct[k])(factor_copy(i, k).wait_send)

    @pl.when(ends)
    def _():
        for i in range(RELAYED, CHUNKS):
            relay_copy(i).wait_send()
            relay_on(i, 0).wait_send()

    total = part[:, pl.ds(pl.multiple_of(x * 32, 32), 32), :]
    for dx in range(1, NX):
        here = parts.at[dx]
        remote(here, here, rs.at[dx], rr.at[dx], after).wait_recv()
        total += parts[dx]
    out[...] = total.astype(BF16)
    for copy in last:
        copy.wait_send()


def body(factors, amplitudes, left_step, right_step, amp_owner, amp_slot):
    dma, any_space = pltpu.SemaphoreType.DMA, pl.BlockSpec(memory_space=pl.ANY)
    terms = left_step.shape[1]
    return pl.pallas_call(
        kernel,
        out_shape=jax.ShapeDtypeStruct((2, 32, W), BF16),
        in_specs=[any_space] * 6,
        out_specs=pl.BlockSpec(memory_space=pltpu.VMEM),
        scratch_shapes=[
            pltpu.VMEM((2, W, W), BF16),
            pltpu.VMEM((4, 2, terms), jnp.int32),
            pltpu.VMEM((2, 8, W), jnp.int32),
            pltpu.VMEM((NY, 16, W), BF16),
            pltpu.VMEM((NY, 32, 256), BF16),
            pltpu.VMEM((NY, 144, 2048), BF16),
            pltpu.VMEM((256, 2048), BF16),
            pltpu.VMEM((NC, NZ, NY, 16, W), BF16),
            pltpu.VMEM((NY, 144, W), BF16),
            pltpu.VMEM((NX * NY, 144, W), BF16),
            pltpu.VMEM((3, 3 * W, 2 * W), BF16),
            pltpu.VMEM((PAUX * W, 3 * W), BF16),
            pltpu.VMEM((2, W, W), F32),
            pltpu.VMEM((NX, 2, 32, W), F32),
            pltpu.VMEM((2, PAUX * W // CHUNKS, 2 * W), BF16),
            pltpu.VMEM((CHUNKS - RELAYED, PAUX * W // CHUNKS, W), BF16),
            dma((8,)),
            dma((12,)), dma((12,)),
            dma((4,)), dma((4,)),
            dma((15,)), dma((15,)),
            dma((16,)), dma((1,)),
            dma((3, 16)), dma((3,)),
            dma((2, CHUNKS)), dma((2, CHUNKS)),
            dma((4,)), dma((4,)),
            dma((CHUNKS - RELAYED,)), dma((CHUNKS - RELAYED,)), dma((CHUNKS - RELAYED,)),
        ],
        compiler_params=pltpu.CompilerParams(
            collective_id=0, has_side_effects=True, vmem_limit_bytes=56 * 2**20
        ),
        cost_estimate=pl.CostEstimate(flops=4 * 10**9, bytes_accessed=4 * 2**20, transcendentals=0),
    )(factors.reshape(PAUX * W, W), amplitudes, left_step, right_step, amp_owner, amp_slot)


def solution(mesh):
    return jax.shard_map(
        body,
        mesh=mesh,
        in_specs=(
            P("tile", "fit", None, None),
            P("tile", None, None),
            P("tile", None),
            P("tile", None),
            P("tile", None),
            P("tile", None),
        ),
        out_specs=P("tile", "fit", None),
        check_vma=False,
    )
```

```python
import jax
import jax.numpy as jnp
from jax import lax
from jax.experimental import pallas as pl
from jax.experimental.pallas import tpu as pltpu
from jax.sharding import PartitionSpec as P

NX, NY, NZ, NC = 4, 4, 16, 2
TILES = NY * NZ * NC
W = 128
PAUX = 32
FAR = (0, 5, -5)
NEAR = (2, -2, 1, -1)
CHUNKS = 4
GROUP = 48
ORDER = (1, 0, 2)
EARLY = 1
RELAYED = 2
BF16, F32 = jnp.bfloat16, jnp.float32


def remote(src, dst, send, recv, device):
    return pltpu.make_async_remote_copy(
        src_ref=src,
        dst_ref=dst,
        send_sem=send,
        recv_sem=recv,
        device_id=device,
        device_id_type=pl.DeviceIdType.MESH,
    )


def kernel(
    fac, amp, lstep, rstep, own, slot, out,
    amp_v, idx_v, code, pack, marks, wide, spread, tiles, picked, landed, amat, fcat, part, parts, halves, via,
    loc, s1s, s1r, ms, mr, s2s, s2r, cs, cr, s4s, s4r, fs, fr, rs, rr, vs, vr, ws,
):
    t = lax.axis_index("tile")
    x = lax.axis_index("fit")
    c = lax.rem(t, NC)
    z = lax.rem(t // NC, NZ)
    y = t // (NC * NZ)

    def at(dx, dy, dz, dc):
        yy, zz = lax.rem(y + dy + NY, NY), lax.rem(z + dz + NZ, NZ)
        return ((yy * NZ + zz) * NC + lax.rem(c + dc, NC), lax.rem(x + dx, NX))

    before = (lax.rem(t + TILES - 1, TILES), x)
    after = (lax.rem(t + 1, TILES), x)
    cross = jnp.where(c == 0, before[0], after[0])
    ends = ((z == 0) & (c == 0)) | ((z == NZ - 1) & (c == 1))
    corner = (y * NZ * NC + jnp.where(c == 0, NZ * NC - 1, 0), x)
    direct = (jnp.logical_not(ends & (c == 1)), jnp.logical_not(ends & (c == 0)))

    barrier = pltpu.get_barrier_semaphore()
    steps = {(0, 0, 0, 1)}
    for dy in range(NY):
        steps |= {(0, dy, dz, 0) for dz in FAR} | {(dx, dy, 0, 0) for dx in range(NX)}
    steps |= {(0, 0, dz, 0) for dz in (1, -1, 2, -2, 3, -3)}
    steps.discard((0, 0, 0, 0))

    def hops(step):
        return (min(step[0], NX - step[0]) + min(step[1], NY - step[1]) + abs(step[2]), step)

    peers = [at(*step) for step in sorted(steps, key=hops, reverse=True)]
    peers.append((cross, x))
    for peer in peers:
        pl.semaphore_signal(barrier, inc=1, device_id=peer, device_id_type=pl.DeviceIdType.MESH)

    @pl.when(ends)
    def _():
        pl.semaphore_signal(barrier, inc=1, device_id=corner, device_id_type=pl.DeviceIdType.MESH)


    loads = [pltpu.make_async_copy(amp, amp_v, loc.at[0])]
    for i, ref in enumerate((lstep, rstep, own, slot)):
        loads.append(pltpu.make_async_copy(ref, idx_v.at[i], loc.at[1 + i]))
    keep = pltpu.make_async_copy(fac, fcat.at[:, pl.ds(W, W)], loc.at[5])
    for copy in loads:
        copy.start()
    keep.start()

    for copy in loads:
        copy.wait()

    rows = amp_v[:, pl.ds(pl.multiple_of(x * 32, 32), 32), :].astype(F32).reshape(2, NY, 8, W)
    for dest in range(NY):
        pack[dest] = rows[:, dest].reshape(16, W).astype(BF16)

    lpos = jnp.clip(t + idx_v[0], 0, TILES - 1) - t + 1
    rpos = jnp.clip(t + idx_v[1], 0, TILES - 1) - t + 1
    owner = idx_v[2]
    tile = ((((owner & 1) ^ c) * NZ + ((owner >> 1) & (NZ - 1))) * NY + (owner >> 5)) * 2 + idx_v[3]
    terms = lpos.shape[1]
    code[...] = jnp.full(code.shape, -1, jnp.int32)
    code[0, 0:2, 0:terms] = lpos * 3 + rpos
    code[1, 0:2, 0:terms] = tile
    for s in range(2):
        block_of = (lax.broadcasted_iota(jnp.int32, (16, W), 0) == code[0, s : s + 1, :]).astype(BF16)
        tile_of = (lax.broadcasted_iota(jnp.int32, (256, W), 0) == code[1, s : s + 1, :]).astype(BF16)
        both = lax.dot_general(block_of, tile_of, (((1,), (1,)), ((), ())), preferred_element_type=F32)
        marks[y, 16 * s : 16 * (s + 1), :] = both.astype(BF16)
    pl.semaphore_wait(barrier, len(peers) + jnp.where(ends, 1, 0))

    count = PAUX * W // CHUNKS

    def factor_copy(i, k):
        part_rows = pl.ds(i * count, count)
        device, lane = ((after, 0), (before, 2 * W))[k]
        return remote(fac.at[part_rows], fcat.at[part_rows, pl.ds(lane, W)], fs.at[k, i], fr.at[k, i], device)

    def start_factors(lo, hi):
        for i in range(lo, hi):
            for k in range(2):
                copy = factor_copy(i, k)
                if i < RELAYED:
                    copy.start()
                    sent.append(copy)
                else:
                    pl.when(direct[k])(copy.start)

    def relay_copy(i):
        dy = jnp.where(c == 1, 1, -1)
        return remote(
            fac.at[pl.ds(i * count, count)], via.at[i - RELAYED], vs.at[i - RELAYED], vr.at[i - RELAYED], at(0, dy, 0, 0)
        )

    def relay_on(i, k):
        dst = fcat.at[pl.ds(i * count, count), pl.ds(2 * W * k, W)]
        return remote(via.at[i - RELAYED], dst, ws.at[i - RELAYED], fr.at[k, i], corner)

    sent = []
    first = {}
    for dz in (5, -5, 0):
        for dy in (2, 1, 3, 0):
            j = FAR.index(dz) * NY + dy
            dst = lax.rem(y + dy, NY)
            if dy or dz:
                first[dz, dy] = remote(pack.at[dst], tiles.at[0, z, y], s1s.at[j], s1r.at[j], at(0, dy, dz, 0))
                first[dz, dy].start()
                sent.append(first[dz, dy])
            else:
                mine = pltpu.make_async_copy(pack.at[dst], tiles.at[0, z, y], loc.at[6])
                mine.start()
    for dy in range(1, NY):
        copy = remote(marks.at[y], marks.at[y], ms.at[dy], mr.at[dy], at(0, dy, 0, 0))
        copy.start()
        sent.append(copy)

    spread[...] = (
        lax.broadcasted_iota(jnp.int32, (256, 2048), 1) // 8 == lax.broadcasted_iota(jnp.int32, (256, 2048), 0)
    ).astype(BF16)

    start_factors(0, EARLY)

    @pl.when(ends)
    def _():
        for i in range(RELAYED, CHUNKS):
            relay_copy(i).start()


    def arrived(dz, dy):
        j = FAR.index(dz) * NY + dy
        zz, yy = lax.rem(z - dz + NZ, NZ), lax.rem(y - dy + NY, NY)
        here = tiles.at[0, zz, yy]
        remote(here, here, s1s.at[j], s1r.at[j], after).wait_recv()

    def tile_block(dz, core=0):
        return tiles.at[core, lax.rem(z - dz + 2 * NZ, NZ)]

    partner = at(0, 0, 0, 1)

    def share(dz):
        j = dz + 7
        copy = remote(tile_block(dz), tile_block(dz, 1), cs.at[j], cr.at[0], partner)
        copy.start()
        sent.append(copy)

    near = []
    for i, dz in enumerate(FAR):
        for dy in range(NY):
            if dy or dz:
                arrived(dz, dy)
        if dz == 0:
            mine.wait()
        steps = ((3,) if dz == 5 else ()) + NEAR
        for k, step in enumerate(steps):
            j = i * 5 + k
            copy = remote(tile_block(dz), tile_block(dz), s2s.at[j], s2r.at[j], at(0, 0, step, 0))
            copy.start()
            sent.append(copy)
            near.append((j, dz + step))
        share(dz)

    start_factors(EARLY, CHUNKS)
    for dy in range(1, NY):
        here = marks.at[lax.rem(y - dy + NY, NY)]
        remote(here, here, ms.at[dy], mr.at[dy], after).wait_recv()
    row = lax.broadcasted_iota(jnp.int32, (144, 32), 0) // 8
    col = lax.broadcasted_iota(jnp.int32, (144, 32), 1)
    rowpick = (row // 6 + 3 * (row % 3) + 16 * ((row // 3) & 1) == col).astype(BF16)
    same = (lax.broadcasted_iota(jnp.int32, (144, 2048), 0) & 7) == (
        lax.broadcasted_iota(jnp.int32, (144, 2048), 1) & 7
    )
    for dest in range(NY):
        blocks = jnp.dot(rowpick, marks[dest], preferred_element_type=F32).astype(BF16)
        full = jnp.dot(blocks, spread[...], preferred_element_type=F32)
        wide[dest] = jnp.where(same, full, 0.0).astype(BF16)

    for j, dz in near:
        remote(tile_block(dz), tile_block(dz), s2s.at[j], s2r.at[j], after).wait_recv()
        share(dz)

    @pl.when(ends)
    def _():
        for i in range(RELAYED, CHUNKS):
            relay_copy(i).wait_recv()
            for k in range(2):
                pl.when(c == 1 - k)(relay_on(i, k).start)

    def picks(g, core):
        marked = wide[:, GROUP * g : GROUP * (g + 1), 1024 * core : 1024 * (core + 1)].reshape(NY * GROUP, 1024)
        return jnp.dot(marked, tiles[core].reshape(1024, W), preferred_element_type=F32)

    own_half = [picks(g, 0) for g in ORDER]
    remote(tiles.at[1], tiles.at[1], cs.at[0], cr.at[0], partner).wait_recv()

    place = x * NY + y

    def group_of(ref, g):
        return ref.at[pl.ds(GROUP * g, GROUP)]

    kept = {}
    for n, g in enumerate(ORDER):
        both = (own_half[n] + picks(g, 1)).astype(BF16)
        picked[:, GROUP * g : GROUP * (g + 1), :] = both.reshape(NY, GROUP, W)
        for dx in (2, 1, 3, 0):
            for dy in (2, 1, 3, 0):
                src_ref, dst_ref = group_of(picked.at[lax.rem(y + dy, NY)], g), group_of(landed.at[place], g)
                j = dx * NY + dy
                if dx or dy:
                    copy = remote(src_ref, dst_ref, s4s.at[g, j], s4r.at[g], at(dx, dy, 0, 0))
                    sent.append(copy)
                else:
                    copy = kept[g] = pltpu.make_async_copy(src_ref, dst_ref, s4s.at[g, 0])
                copy.start()

    def blocks_here(g):
        kept[g].wait()
        others = landed.at[pl.ds(0, NX * NY - 1), pl.ds(GROUP * g, GROUP)]
        remote(others, others, s4s.at[g, 1], s4r.at[g], after).wait_recv()
        for j in range(0, 6, 2):
            lo = GROUP * g + 8 * j
            both = landed[:, lo : lo + 16, :].astype(F32)
            for k in range(2):
                s, left = divmod(j + k, 3)
                block = both[:, 8 * k : 8 * k + 8, :].reshape(W, W).astype(BF16)
                amat[g, pl.ds(left * W, W), pl.ds(s * W, W)] = block

    def factors_here(i):
        for k, lane in enumerate((0, 2 * W)):
            here = fcat.at[pl.ds(i * count, count), pl.ds(lane, W)]
            remote(fac.at[pl.ds(i * count, count)], here, fs.at[k, i], fr.at[k, i], after).wait_recv()

    def right_products(i, g):
        halves[i % 2] = jnp.dot(fcat[pl.ds(i * count, count), :], amat[g], preferred_element_type=F32).astype(BF16)

    def left_products(i, g):
        half, block = halves[i % 2], fcat[pl.ds(i * count, count), g * W : (g + 1) * W]
        steps = range(0, count, W)
        right = jnp.concatenate([block[p : p + W] for p in steps], axis=1)
        for s in range(2):
            left = jnp.concatenate([half[p : p + W, s * W : (s + 1) * W] for p in steps], axis=1)
            part[s] += lax.dot_general(left, right, (((1,), (1,)), ((), ())), preferred_element_type=F32)

    keep.wait()
    part[...] = jnp.zeros(part.shape, F32)
    todo = [(i, g) for g in ORDER for i in range(CHUNKS)]
    for n, (i, g) in enumerate(todo):
        if i == 0:
            blocks_here(g)
        if g == ORDER[0]:
            factors_here(i)
        right_products(i, g)
        if n:
            left_products(*todo[n - 1])
    left_products(*todo[-1])

    last = []
    for dx in (2, 1, 3):
        rows = pl.ds(pl.multiple_of(lax.rem(x + dx, NX) * 32, 32), 32)
        copy = remote(part.at[:, rows], parts.at[dx], rs.at[dx], rr.at[dx], at(dx, 0, 0, 0))
        copy.start()
        last.append(copy)
    for copy in sent:
        copy.wait_send()
    for i in range(RELAYED, CHUNKS):
        for k in range(2):
            pl.when(direct[k])(factor_copy(i, k).wait_send)

    @pl.when(ends)
    def _():
        for i in range(RELAYED, CHUNKS):
            relay_copy(i).wait_send()
            relay_on(i, 0).wait_send()

    total = part[:, pl.ds(pl.multiple_of(x * 32, 32), 32), :]
    for dx in range(1, NX):
        here = parts.at[dx]
        remote(here, here, rs.at[dx], rr.at[dx], after).wait_recv()
        total += parts[dx]
    out[...] = total.astype(BF16)
    for copy in last:
        copy.wait_send()


def body(factors, amplitudes, left_step, right_step, amp_owner, amp_slot):
    dma, any_space = pltpu.SemaphoreType.DMA, pl.BlockSpec(memory_space=pl.ANY)
    terms = left_step.shape[1]
    return pl.pallas_call(
        kernel,
        out_shape=jax.ShapeDtypeStruct((2, 32, W), BF16),
        in_specs=[any_space] * 6,
        out_specs=pl.BlockSpec(memory_space=pltpu.VMEM),
        scratch_shapes=[
            pltpu.VMEM((2, W, W), BF16),
            pltpu.VMEM((4, 2, terms), jnp.int32),
            pltpu.VMEM((2, 8, W), jnp.int32),
            pltpu.VMEM((NY, 16, W), BF16),
            pltpu.VMEM((NY, 32, 256), BF16),
            pltpu.VMEM((NY, 144, 2048), BF16),
            pltpu.VMEM((256, 2048), BF16),
            pltpu.VMEM((NC, NZ, NY, 16, W), BF16),
            pltpu.VMEM((NY, 144, W), BF16),
            pltpu.VMEM((NX * NY, 144, W), BF16),
            pltpu.VMEM((3, 3 * W, 2 * W), BF16),
            pltpu.VMEM((PAUX * W, 3 * W), BF16),
            pltpu.VMEM((2, W, W), F32),
            pltpu.VMEM((NX, 2, 32, W), F32),
            pltpu.VMEM((2, PAUX * W // CHUNKS, 2 * W), BF16),
            pltpu.VMEM((CHUNKS - RELAYED, PAUX * W // CHUNKS, W), BF16),
            dma((8,)),
            dma((12,)), dma((12,)),
            dma((4,)), dma((4,)),
            dma((15,)), dma((15,)),
            dma((16,)), dma((1,)),
            dma((3, 16)), dma((3,)),
            dma((2, CHUNKS)), dma((2, CHUNKS)),
            dma((4,)), dma((4,)),
            dma((CHUNKS - RELAYED,)), dma((CHUNKS - RELAYED,)), dma((CHUNKS - RELAYED,)),
        ],
        compiler_params=pltpu.CompilerParams(
            collective_id=0, has_side_effects=True, vmem_limit_bytes=56 * 2**20
        ),
        cost_estimate=pl.CostEstimate(flops=4 * 10**9, bytes_accessed=4 * 2**20, transcendentals=0),
    )(factors.reshape(PAUX * W, W), amplitudes, left_step, right_step, amp_owner, amp_slot)


def solution(mesh):
    return jax.shard_map(
        body,
        mesh=mesh,
        in_specs=(
            P("tile", "fit", None, None),
            P("tile", None, None),
            P("tile", None),
            P("tile", None),
            P("tile", None),
            P("tile", None),
        ),
        out_specs=P("tile", "fit", None),
        check_vma=False,
    )
```
